512 devices in a mesh: pb: 32 (over x, z_hi, core), row: 16 (over y, z_lo).
Axes of the slice: x: 4, y: 4, z: 16 (z_hi: 4, z_lo: 4; z = z_hi * 4 + z_lo), core: 2. Of those that a mesh axis runs over, the one named last changes fastest.
Arguments:
- dec_states: bfloat16 [32, 64, 2048], P('pb'), may hold values from -6 to 6
- enc_states: bfloat16 [32, 2048, 2048], P('pb', 'row'), may hold values from -6 to 6
- passage_lengths: int32 [32, 16], P('pb'), may hold values from 1 to 128, as said below
- q_weight: bfloat16 [2048, 4096], P('pb', 'row'), may hold values from -0.125 to 0.125
- kv_weight: bfloat16 [2048, 256], P('pb'), may hold values from -0.125 to 0.125
- o_weight: bfloat16 [4096, 2048], P('row', 'pb'), may hold values from -0.09375 to 0.09375
- out_grad: bfloat16 [32, 64, 2048], P('pb'), may hold values from -192 to 192
Outputs:
- dec_grad: bfloat16 [32, 64, 2048], P('pb', None, 'row')
- enc_grad: bfloat16 [32, 2048, 2048], P('pb', 'row')
- q_weight_grad: float32 [2048, 4096], P(None, 'row')
- kv_weight_grad: float32 [2048, 256], P('pb')
- o_weight_grad: bfloat16 [4096, 2048], P('row')
The draws below stay inside these ranges and needn't reach their ends.
Inputs may be any that keep to these rules, and one draw needn't show every extreme that they name: passage_lengths[q, p] counts the real tokens at the start of passage p of question q; every question has a passage of full length 128.
All inputs are finite; a program needn't handle non-finite values.
Results may differ from the reference program's by a relative error of at most 0.034.
Values may be sent and summed in bfloat16 or wider, within the bound.
No kernel may reach another device: no remote copies, remote signals or barrier semaphores. Data moves between devices by JAX's collectives and lax.ppermute only.
A program may use at most 64 MiB of HBM per device.

```python
import jax
import jax.numpy as jnp
from jax import lax

D = 2048
HEADS = 32
HD = 128
PT = 128
A = 64
QUESTIONS = 32
NPASS = 16
KEYS = 2048
N_ROW = 16


def draw_passage_lengths(key, part):
    key = jax.random.fold_in(key, 7)
    first_key, second_key = jax.random.split(key)
    drawn_len = jax.random.randint(first_key, (QUESTIONS, NPASS), 1, PT + 1)
    full_slot = jax.random.randint(second_key, (QUESTIONS, 1), 0, NPASS)
    return jnp.where(jnp.arange(NPASS)[None, :] == full_slot, PT, drawn_len).astype(jnp.int32)


def block_levels(own_key, shape, shards, low, high):
    loudness, own = 1.0, jax.random.fold_in(own_key, 6)
    for axis_at, parts in shards:
        draws = jnp.exp(jax.random.uniform(jax.random.fold_in(own, axis_at), (parts,), jnp.float32, low / len(shards), high / len(shards)))
        loudness = loudness * jnp.repeat(draws, shape[axis_at] // parts).reshape([-1 if axis == axis_at else 1 for axis in range(len(shape))])
    return loudness


def bell_draw(rng, shape, scale, reach, shards=(), kind=jnp.bfloat16):
    array = scale * jax.random.normal(rng, shape, jnp.float32)
    if shards:
        array = array * block_levels(rng, shape, shards, -0.22, 0.18)
    return jnp.clip(array, -reach, reach).astype(kind)


def setup_inputs(seed: int = 0) -> dict:
    arg_keys = jax.random.split(jax.random.key(seed), 8)
    return {
        "dec_states": bell_draw(arg_keys[0], (QUESTIONS, A, D), 1.0, 6.0, ((0, 32),)),
        "enc_states": bell_draw(arg_keys[1], (QUESTIONS, KEYS, D), 1.0, 6.0, ((0, 32), (1, 16))),
        "passage_lengths": draw_passage_lengths(jax.random.fold_in(arg_keys[7], 71), 0),
        "q_weight": bell_draw(arg_keys[3], (D, HEADS * HD), D ** -0.5, 0.125, ((0, 32), (1, 16))),
        "kv_weight": bell_draw(arg_keys[4], (D, 2 * HD), D ** -0.5, 0.125, ((0, 32),)),
        "o_weight": bell_draw(arg_keys[5], (HEADS * HD, D), (HEADS * HD) ** -0.5, 0.09375, ((0, 16), (1, 32))),
        "out_grad": bell_draw(arg_keys[6], (QUESTIONS, A, D), 32.0, 192.0, ((0, 32),)),
    }


def round_keep(term):
    return lax.optimization_barrier(term.astype(jnp.bfloat16)).astype(jnp.float32)


def one_question(dec_rows, enc_rows, length_row, grad_rows, q_weight, kv_weight, o_weight):
    f32 = jnp.float32
    score_scale = HD ** -0.5
    row_count = dec_rows.shape[0]
    queries = jnp.dot(dec_rows, q_weight, preferred_element_type=f32).astype(jnp.bfloat16)
    key_values = jnp.dot(enc_rows, kv_weight, preferred_element_type=f32).astype(jnp.bfloat16)
    key_rows = key_values[:, :HD].astype(f32)
    value_rows = key_values[:, HD:].astype(f32)
    valid_mask = (jnp.arange(PT)[None, :] < length_row[:, None]).reshape(-1)
    query_heads = queries.reshape(row_count, HEADS, HD).astype(f32)
    scores = jnp.einsum('ahd,td->hat', query_heads, key_rows) * score_scale
    weights = jnp.where(valid_mask[None, None, :], jnp.exp(scores), 0.0)
    totals = jnp.sum(weights, -1)
    weights_b = weights.astype(jnp.bfloat16).astype(f32)
    mixed = jnp.einsum('hat,td->ahd', weights_b, value_rows) / totals.T[:, :, None]
    mixed_b = mixed.reshape(row_count, HEADS * HD).astype(jnp.bfloat16)
    attn_grad = jnp.dot(grad_rows, o_weight.T, preferred_element_type=f32).astype(jnp.bfloat16)
    o_term = round_keep(jnp.dot(mixed_b.T, grad_rows, preferred_element_type=f32))
    grad_heads = attn_grad.reshape(row_count, HEADS, HD).astype(f32)
    probs = weights / totals[..., None]
    dprob = jnp.einsum('ahd,td->hat', grad_heads, value_rows)
    delta_rows = jnp.sum(grad_heads * mixed, -1).T
    dscore = probs * (dprob - delta_rows[..., None]) * score_scale
    dscore_b = dscore.astype(jnp.bfloat16).astype(f32)
    probs_b = probs.astype(jnp.bfloat16).astype(f32)
    query_grad = jnp.einsum('hat,td->ahd', dscore_b, key_rows).reshape(row_count, HEADS * HD).astype(jnp.bfloat16)
    group_heads = HEADS // N_ROW
    key_parts = jnp.einsum('gcat,agcd->gtd', dscore_b.reshape(N_ROW, group_heads, row_count, -1), query_heads.reshape(row_count, N_ROW, group_heads, HD))
    value_parts = jnp.einsum('gcat,agcd->gtd', probs_b.reshape(N_ROW, group_heads, row_count, -1), grad_heads.reshape(row_count, N_ROW, group_heads, HD))
    key_grad = jnp.sum(round_keep(key_parts), 0)
    value_grad = jnp.sum(round_keep(value_parts), 0)
    kv_grad = jnp.concatenate([key_grad, value_grad], -1).astype(jnp.bfloat16)
    enc_grad = jnp.dot(kv_grad, kv_weight.T, preferred_element_type=f32).astype(jnp.bfloat16)
    kv_term = jnp.dot(enc_rows.T, kv_grad, preferred_element_type=f32)
    q_term = round_keep(jnp.dot(dec_rows.T, query_grad, preferred_element_type=f32))
    dec_grad = jnp.dot(query_grad, q_weight.T, preferred_element_type=f32).astype(jnp.bfloat16)
    return dec_grad, enc_grad, q_term, kv_term, o_term


def reference(dec_states, enc_states, passage_lengths, q_weight, kv_weight, o_weight, out_grad):
    def step_fn(carry, items):
        q_total, kv_total, o_total = carry
        dec_grad, enc_grad, q_term, kv_term, o_term = one_question(items[0], items[1], items[2], items[3], q_weight, kv_weight, o_weight)
        return (q_total + q_term, kv_total + kv_term, o_total + o_term), (dec_grad, enc_grad)

    start_carry = (jnp.zeros(q_weight.shape, jnp.float32), jnp.zeros(kv_weight.shape, jnp.float32), jnp.zeros(o_weight.shape, jnp.float32))
    totals_end, per_question = lax.scan(step_fn, start_carry, (dec_states, enc_states, passage_lengths, out_grad))
    return per_question[0], per_question[1], totals_end[0], totals_end[1], totals_end[2].astype(jnp.bfloat16)
```

```python
import jax
import jax.numpy as jnp
from jax import lax
from jax.sharding import Mesh, PartitionSpec as P

HD = 128
PT = 128
f32 = jnp.float32
bf16 = jnp.bfloat16


def spread(block, axis, count):
    copies = jnp.broadcast_to(block[None], (count,) + block.shape)
    return lax.all_to_all(copies, axis, 0, 0)


def exchange(parts, axis):
    return jnp.sum(lax.all_to_all(parts, axis, 0, 0).astype(f32), 0)


def swap(block):
    return lax.ppermute(block, "co", [(0, 1), (1, 0)])


def local(dec_states, enc_states, passage_lengths, q_weight, kv_weight, o_weight, out_grad):
    score_scale = HD ** (-0.5)
    dec_rows = dec_states[0]
    enc_rows = enc_states[0]
    grad_rows = out_grad[0]
    co = lax.axis_index("co")
    zl = lax.axis_index("zl")
    first_core = co == 0

    shard = jnp.concatenate([q_weight, kv_weight, o_weight.T], 1)
    own = lax.all_gather(shard, "zh", axis=0, tiled=True)
    own = spread(own, "x", 4).reshape(16, 64, 768)
    other = swap(own)
    weights_all = jnp.stack(
        [jnp.where(first_core, own, other), jnp.where(first_core, other, own)], 1
    ).reshape(2048, 768)
    wq_full = weights_all[:, :256]
    wkv_full = weights_all[:, 256:512]
    wo_t = weights_all[:, 512:]

    key_values = jnp.dot(enc_rows, wkv_full, preferred_element_type=f32).astype(bf16)
    queries = jnp.dot(dec_rows, wq_full, preferred_element_type=f32).astype(bf16)
    attn_grad = jnp.dot(grad_rows, wo_t, preferred_element_type=f32).astype(bf16)

    kv_all = spread(key_values, "y", 4).reshape(512, 256)
    qa_all = spread(jnp.concatenate([queries, attn_grad], 1), "zl", 4)
    key_rows = kv_all[:, :HD]
    value_rows = kv_all[:, HD:]
    query_heads = qa_all[:, :, :256].reshape(4, 64, 2, HD)
    grad_heads = qa_all[:, :, 256:].reshape(4, 64, 2, HD)
    lengths = lax.dynamic_index_in_dim(passage_lengths[0].reshape(4, 4), zl, 1, keepdims=False)
    valid_mask = (jnp.arange(PT)[None, :] < lengths[:, None]).reshape(-1)

    scores = jnp.einsum("zacd,td->zcat", query_heads, key_rows, preferred_element_type=f32)
    weights = jnp.where(valid_mask, jnp.exp(scores * score_scale), 0.0)
    dprob = jnp.einsum("zacd,td->zcat", grad_heads, value_rows, preferred_element_type=f32)
    part_total = jnp.sum(weights, -1)
    part_safe = jnp.where(part_total > 0, part_total, 1.0)
    part_delta = jnp.sum(weights / part_safe[..., None] * dprob, -1)
    stats = spread(jnp.stack([part_total, part_delta]).reshape(8, 128), "zl", 4)
    stats = stats.reshape(4, 2, 4, 2, 64)
    totals = jnp.sum(stats[:, 0], 0)
    delta = jnp.sum(stats[:, 0] / totals * stats[:, 1], 0)
    weights_b = weights.astype(bf16)
    probs = weights / totals[..., None]
    dscore_b = (probs * (dprob - delta[..., None]) * score_scale).astype(bf16)
    probs_b = probs.astype(bf16)
    mixed_part = jnp.einsum(
        "zcat,td->zacd", weights_b, value_rows, preferred_element_type=f32
    ) / totals.transpose(0, 2, 1)[..., None]
    query_part = jnp.einsum("zcat,td->zacd", dscore_b, key_rows, preferred_element_type=f32)
    own_parts = jnp.concatenate(
        [mixed_part.reshape(4, 64, 256), query_part.reshape(4, 64, 256)], 2
    ).astype(bf16)
    own_heads = exchange(own_parts, "zl").astype(bf16)
    mixed_own = own_heads[:, :256]
    query_grad = own_heads[:, 256:]

    key_part = jnp.einsum("zcat,zacd->td", dscore_b, query_heads, preferred_element_type=f32)
    value_part = jnp.einsum("zcat,zacd->td", probs_b, grad_heads, preferred_element_type=f32)
    kv_part = jnp.concatenate([key_part, value_part], -1).astype(bf16).reshape(4, PT, 256)
    dec_part = jnp.dot(query_grad, wq_full.T, preferred_element_type=f32).astype(bf16)
    dec_part = dec_part.reshape(64, 4, 2, 256).transpose(1, 2, 0, 3).reshape(4, 128, 256)
    y_sum = exchange(jnp.concatenate([kv_part, dec_part], 1), "y").astype(bf16)
    kv_grad = y_sum[:PT]
    dec_half = y_sum[PT:].reshape(2, 64, 2, 128).transpose(0, 2, 1, 3).reshape(4, 64, 128)
    dec_grad = exchange(dec_half, "zl").astype(bf16)
    enc_grad = jnp.dot(kv_grad, wkv_full.T, preferred_element_type=f32).astype(bf16)

    q_term = jnp.dot(dec_rows.T, query_grad, preferred_element_type=f32).astype(bf16)
    o_term = jnp.dot(grad_rows.T, mixed_own, preferred_element_type=f32).astype(bf16)
    kv_term = jnp.dot(enc_rows.T, kv_grad, preferred_element_type=f32).astype(bf16)
    kv_term = kv_term.reshape(16, 2, 64, 256).transpose(1, 0, 2, 3).reshape(2, 1024, 256)
    terms = jnp.concatenate(
        [q_term.reshape(2, 1024, 256), o_term.reshape(2, 1024, 256), kv_term], 2
    )
    keep = jnp.where(first_core, terms[0], terms[1])
    send = jnp.where(first_core, terms[1], terms[0])
    chip_sum = (keep.astype(f32) + swap(send).astype(f32)).astype(bf16)
    x_sum = exchange(chip_sum.reshape(4, 256, 768), "x").astype(bf16)
    z_sum = exchange(x_sum.reshape(4, 64, 768), "zh").astype(bf16)
    kv_y = jnp.sum(spread(z_sum[:, 512:], "y", 4).astype(f32), 0).astype(bf16)
    kv_weight_grad = jnp.sum(spread(kv_y, "zl", 4).astype(f32), 0)

    mine = lax.all_gather(z_sum[:, :512], "zh", axis=0, tiled=True)
    mine = spread(mine, "x", 4).reshape(1024, 512)
    theirs = swap(mine)
    both = jnp.concatenate(
        [jnp.where(first_core, mine, theirs), jnp.where(first_core, theirs, mine)], 0
    )
    q_weight_grad = both[:, :256].astype(f32)
    o_weight_grad = both[:, 256:].T
    return (dec_grad[None], enc_grad[None], q_weight_grad, kv_weight_grad, o_weight_grad)


def solution(mesh):
    fine = Mesh(mesh.devices.reshape(4, 4, 2, 4, 4), ("x", "zh", "co", "y", "zl"))
    pb = ("x", "zh", "co")
    row = ("y", "zl")
    placed = (
        P(pb, None, None),
        P(pb, row, None),
        P(pb, None),
        P(pb, row),
        P(pb, None),
        P(row, pb),
        P(pb, None, None),
    )
    return jax.shard_map(
        local,
        mesh=fine,
        in_specs=placed,
        out_specs=(
            P(pb, None, row),
            P(pb, row, None),
            P(None, row),
            P(pb, None),
            P(row, None),
        ),
        check_vma=False,
    )
```

```python
import jax
import jax.numpy as jnp
from jax import lax
from jax.experimental import pallas as pl
from jax.experimental.pallas import tpu as pltpu
from jax.sharding import Mesh, PartitionSpec as P

HD = 128
PT = 128
SCALE = HD ** (-0.5)
f32 = jnp.float32
bf16 = jnp.bfloat16


def spread(block, axis):
    copies = jnp.broadcast_to(block[None], (4,) + block.shape)
    return lax.all_to_all(copies, axis, 0, 0)


def exchange(parts, axis):
    return jnp.sum(lax.all_to_all(parts, axis, 0, 0).astype(f32), 0).astype(bf16)


def swap(block):
    return lax.ppermute(block, "co", [(0, 1), (1, 0)])


def meet(block, axis, bit):
    return lax.ppermute(block, axis, [(i, i ^ bit) for i in range(4)])


def join(keep, moved):
    return (keep.astype(f32) + moved.astype(f32)).astype(bf16)


def halve(parts, axis):
    me = lax.axis_index(axis)
    high, low = me // 2, lax.rem(me, 2)
    keep = lax.dynamic_slice_in_dim(parts, 2 * high, 2, 0)
    send = lax.dynamic_slice_in_dim(parts, 2 - 2 * high, 2, 0)
    two = join(keep, meet(send, axis, 2))
    keep = lax.dynamic_index_in_dim(two, low, 0, keepdims=False)
    send = lax.dynamic_index_in_dim(two, 1 - low, 0, keepdims=False)
    return join(keep, meet(send, axis, 1))


def together(*arrays):
    return lax.optimization_barrier(arrays)


def outer(left, right):
    return lax.dot_general(left, right, (((0,), (0,)), ((), ())), preferred_element_type=f32)


def rows_by_rows(left, right):
    return lax.dot_general(left, right, (((1,), (1,)), ((), ())), preferred_element_type=f32)


def attend(lengths, qa, kv):
    heads = [(z, c) for z in range(4) for c in range(2)]
    q = jnp.concatenate([qa[z, :, c * HD : c * HD + HD] for z, c in heads], 0)
    g = jnp.concatenate([qa[z, :, 256 + c * HD : 256 + c * HD + HD] for z, c in heads], 0)
    token = lax.broadcasted_iota(jnp.int32, (1, 512), 1)
    limit = jnp.full((1, 512), lengths[3], jnp.int32)
    for y in range(2, -1, -1):
        limit = jnp.where(token < PT * (y + 1), lengths[y], limit)
    valid = (token & (PT - 1)) < limit
    scores = rows_by_rows(q, kv[:, :HD]) * SCALE
    weights = jnp.where(valid, jnp.exp(scores), 0.0)
    return q, g, weights, rows_by_rows(g, kv[:, HD:])


def forward_kernel(lengths, qa, kv, out):
    _, _, weights, dprob = attend(lengths, qa, kv)
    total = jnp.sum(weights, -1, keepdims=True)
    probs = weights * (1.0 / jnp.where(total > 0, total, 1.0))
    delta = jnp.sum(probs * dprob, -1, keepdims=True)
    centred = (probs * (dprob - delta)).astype(bf16)
    plain = jnp.dot(probs.astype(bf16), kv[...], preferred_element_type=f32).astype(bf16)
    slope = jnp.dot(centred, kv[:, :HD], preferred_element_type=f32).astype(bf16)
    lane = lax.broadcasted_iota(jnp.int32, (64, 128), 1)
    stats = jnp.zeros((64, 128), f32)
    columns = []
    for h in range(8):
        rows = slice(64 * h, 64 * h + 64)
        for value in (total[rows], delta[rows]):
            high = value.astype(bf16).astype(f32)
            columns += [high, value - high]
    for k, column in enumerate(columns):
        stats = jnp.where(lane == k, column, stats)
    for z in range(4):
        own = stats
        for k in range(8):
            own = jnp.where(lane == 32 + k, columns[8 * z + k], own)
        for c in range(2):
            rows = slice(128 * z + 64 * c, 128 * z + 64 * c + 64)
            out[z, :, c * HD : c * HD + HD] = slope[rows]
            out[z, :, 256 + c * HD : 256 + c * HD + HD] = plain[rows, :HD]
            out[z, :, 512 + c * HD : 512 + c * HD + HD] = plain[rows, HD:]
        out[z, :, 768:] = own.astype(bf16)


def combine(stats, k):
    totals = [s[:, k : k + 1] + s[:, k + 1 : k + 2] for s in stats]
    deltas = [s[:, k + 2 : k + 3] + s[:, k + 3 : k + 4] for s in stats]
    total = totals[0] + totals[1] + totals[2] + totals[3]
    shares = [t / total for t in totals]
    delta = sum(share * d for share, d in zip(shares, deltas))
    return total, delta, shares, deltas


def backward_kernel(lengths, moved, qa, kv, heads, kv_part):
    stats = [moved[i, :, 768:].astype(f32) for i in range(4)]
    for c in range(2):
        _, delta, shares, deltas = combine(stats, 32 + 4 * c)
        mixed = jnp.zeros((64, HD), f32)
        grad = jnp.zeros((64, HD), f32)
        for i in range(4):
            slope, key_mean, value_mean = (
                moved[i, :, at + c * HD : at + c * HD + HD].astype(f32) for at in (0, 256, 512)
            )
            mixed = mixed + shares[i] * value_mean
            grad = grad + shares[i] * (slope + (deltas[i] - delta) * key_mean)
        heads[:64, c * HD : c * HD + HD] = mixed.astype(bf16)
        heads[64:, c * HD : c * HD + HD] = (grad * SCALE).astype(bf16)
    pairs = [combine(stats, 4 * h)[:2] for h in range(8)]
    total = jnp.concatenate([pair[0] for pair in pairs], 0)
    delta = jnp.concatenate([pair[1] for pair in pairs], 0)
    q, g, weights, dprob = attend(lengths, qa, kv)
    probs = weights * (1.0 / total)
    dscore = (probs * (dprob - delta) * SCALE).astype(bf16)
    key_part = outer(dscore, q).astype(bf16)
    value_part = outer(probs.astype(bf16), g).astype(bf16)
    kv_part[:, :HD] = key_part
    kv_part[:, HD:] = value_part


def key_term_kernel(core, kv_part, enc, keep, send):
    term = outer(enc[...], kv_part[...]).astype(bf16).reshape(16, 2, 64, 256)
    at_first = core[0] == 0
    keep[...] = jnp.where(at_first, term[:, 0], term[:, 1])
    send[...] = jnp.where(at_first, term[:, 1], term[:, 0])


def head_term_kernel(sources, moved, own, second, third, fourth, keep, send, kv_sum):
    q_term = o_term = jnp.zeros((512, 256), f32)
    kv_total = jnp.zeros((256, 256), f32)
    for step, rows in enumerate((own, second, third, fourth)):
        block = moved[sources[1 + step]]
        o_term = o_term + outer(rows[:, 512:], block[:64])
        q_term = q_term + outer(rows[:, :512], block[64:128])
        kv_total = kv_total + block[128:].astype(f32)
    term = jnp.concatenate([q_term, o_term], 1).astype(bf16)
    at_first = sources[0] == 0
    keep[...] = jnp.where(at_first, term[:256], term[256:])
    send[...] = jnp.where(at_first, term[256:], term[:256])
    kv_sum[...] = kv_total.astype(bf16)


def place_kernel(core, mine, theirs, q_out, o_out):
    at_first = core[0] == 0
    for half in range(2):
        block = jnp.where(at_first == (half == 0), mine[0], theirs[0])
        q_out[256 * half : 256 * half + 256, :] = block[:, :256].astype(f32)
        o_out[:, 256 * half : 256 * half + 256] = block[:, 256:].T


PARAMS = pltpu.CompilerParams(vmem_limit_bytes=16 * 1024 * 1024)
SCALARS = pl.BlockSpec(memory_space=pltpu.SMEM)


def call(kernel, outs, scalars, *arrays):
    vmem = pl.BlockSpec(memory_space=pltpu.VMEM)
    return pl.pallas_call(
        kernel,
        out_shape=[jax.ShapeDtypeStruct(shape, bf16) for shape in outs],
        in_specs=[SCALARS] + [vmem] * len(arrays),
        out_specs=[vmem] * len(outs),
        compiler_params=PARAMS,
    )(scalars, *arrays)


def place(core, mine, theirs):
    block = pl.BlockSpec((1, 256, 512), lambda i: (i, 0, 0))
    return pl.pallas_call(
        place_kernel,
        grid=(4,),
        out_shape=[
            jax.ShapeDtypeStruct((2048, 256), f32),
            jax.ShapeDtypeStruct((256, 2048), bf16),
        ],
        in_specs=[SCALARS, block, block],
        out_specs=[
            pl.BlockSpec((512, 256), lambda i: (i, 0)),
            pl.BlockSpec((256, 512), lambda i: (0, i)),
        ],
        compiler_params=PARAMS,
    )(core, mine, theirs)


def local(dec_states, enc_states, passage_lengths, q_weight, kv_weight, o_weight, out_grad):
    dec_rows = dec_states[0]
    enc_rows = enc_states[0]
    grad_rows = out_grad[0]
    core = lax.axis_index("co").astype(jnp.int32).reshape(1)
    first_core = lax.axis_index("co") == 0
    zl = lax.axis_index("zl")
    lengths = lax.dynamic_index_in_dim(passage_lengths[0].reshape(4, 4), zl, 1, keepdims=False)

    enc_four = spread(enc_rows, "y").reshape(512, 2048)

    shard = jnp.concatenate([q_weight, kv_weight, o_weight.T], 1)
    own = lax.all_gather(shard, "zh", axis=0, tiled=True)
    own, enc_four = together(own, enc_four)
    own = spread(own, "x").reshape(16, 64, 768)
    other = swap(own)
    weights_all = jnp.stack(
        [jnp.where(first_core, own, other), jnp.where(first_core, other, own)], 1
    ).reshape(2048, 768)
    wq_full = weights_all[:, :256]
    wkv_full = weights_all[:, 256:512]
    wo_t = weights_all[:, 512:]

    queries = jnp.dot(dec_rows, wq_full, preferred_element_type=f32).astype(bf16)
    attn_grad = jnp.dot(grad_rows, wo_t, preferred_element_type=f32).astype(bf16)

    qa_all = spread(jnp.concatenate([queries, attn_grad], 1), "zl")
    kv_all = jnp.dot(enc_four, wkv_full, preferred_element_type=f32).astype(bf16)
    (parts,) = call(forward_kernel, [(4, 64, 896)], lengths, qa_all, kv_all)

    quarters = jnp.stack(
        [
            jnp.concatenate([dec_rows[:, at : at + 512], grad_rows[:, at : at + 512]], 1)
            for at in range(0, 2048, 512)
        ]
    )
    parts, quarters = together(parts, quarters)
    moved = lax.all_to_all(parts, "zl", 0, 0)
    x = lax.axis_index("x")
    rows_x = [lax.dynamic_index_in_dim(quarters, x, 0, keepdims=False)]
    for step in range(1, 4):
        part = lax.dynamic_index_in_dim(quarters, lax.rem(x + step, 4), 0, keepdims=False)
        rows_x.append(lax.ppermute(part, "x", [(i, (i + step) % 4) for i in range(4)]))
    moved, *rows_x = together(moved, *rows_x)
    heads, kv_part = call(backward_kernel, [(128, 256), (512, 256)], lengths, moved, qa_all, kv_all)

    keep, send = call(key_term_kernel, [(16, 64, 256)] * 2, core, kv_part, enc_four)
    kv_chip = join(keep, swap(send)).reshape(4, 256, 256)
    messages = jnp.concatenate([jnp.broadcast_to(heads[None], (4, 128, 256)), kv_chip], 1)
    moved_x = lax.all_to_all(messages, "x", 0, 0)
    sources = jnp.concatenate([core] + [lax.rem(x + 4 - step, 4).reshape(1) for step in range(4)])
    keep, send, kv_sum = call(
        head_term_kernel, [(256, 512), (256, 512), (256, 256)], sources, moved_x, *rows_x
    )
    sum_x = jnp.concatenate([join(keep, swap(send)), kv_sum], 1)
    parts_z = sum_x.reshape(4, 64, 768)

    dec_part = jnp.dot(heads[64:], wq_full.T, preferred_element_type=f32).astype(bf16)
    dec_part = dec_part.reshape(64, 4, 2, 256).transpose(1, 2, 0, 3).reshape(4, 128, 256)
    y_sum = halve(jnp.concatenate([kv_part.reshape(4, PT, 256), dec_part], 1), "y")
    kv_grad = y_sum[:PT]
    dec_y = y_sum[PT:].reshape(2, 64, 2, 128).transpose(0, 2, 1, 3).reshape(4, 64, 128)
    dec_grad = halve(dec_y, "zl")
    enc_grad = jnp.dot(kv_grad, wkv_full.T, preferred_element_type=f32).astype(bf16)

    sum_z = exchange(parts_z, "zh")
    sum_z, dec_grad, enc_grad = together(sum_z, dec_grad, enc_grad)

    kv_y = jnp.sum(spread(sum_z[:, 512:], "y").astype(f32), 0).astype(bf16)
    mine = lax.all_gather(sum_z[:, :512], "zh", axis=0, tiled=True)
    mine, kv_y = together(mine, kv_y)
    mine = spread(mine, "x")
    kv_weight_grad = jnp.sum(lax.all_gather(kv_y, "zl", axis=0).astype(f32), 0)
    mine, kv_weight_grad = together(mine, kv_weight_grad)
    q_weight_grad, o_weight_grad = place(core, mine, swap(mine))
    return (dec_grad[None], enc_grad[None], q_weight_grad, kv_weight_grad, o_weight_grad)


def solution(mesh):
    fine = Mesh(mesh.devices.reshape(4, 4, 2, 4, 4), ("x", "zh", "co", "y", "zl"))
    pb = ("x", "zh", "co")
    row = ("y", "zl")
    placed = (
        P(pb, None, None),
        P(pb, row, None),
        P(pb, None),
        P(pb, row),
        P(pb, None),
        P(row, pb),
        P(pb, None, None),
    )
    return jax.shard_map(
        local,
        mesh=fine,
        in_specs=placed,
        out_specs=(
            P(pb, None, row),
            P(pb, row, None),
            P(None, row),
            P(pb, None),
            P(row, None),
        ),
        check_vma=False,
    )
```

```python
import jax
import jax.numpy as jnp
from jax import lax
from jax.experimental import pallas as pl
from jax.experimental.pallas import tpu as pltpu
from jax.sharding import Mesh, PartitionSpec as P

HD = 128
PT = 128
SCALE = HD ** (-0.5)
f32 = jnp.float32
bf16 = jnp.bfloat16


def spread(block, axis):
    copies = jnp.broadcast_to(block[None], (4,) + block.shape)
    return lax.all_to_all(copies, axis, 0, 0)


def exchange(parts, axis):
    return jnp.sum(lax.all_to_all(parts, axis, 0, 0).astype(f32), 0).astype(bf16)


def swap(block):
    return lax.ppermute(block, "co", [(0, 1), (1, 0)])


def meet(block, axis, bit):
    return lax.ppermute(block, axis, [(i, i ^ bit) for i in range(4)])


def join(keep, moved):
    return (keep.astype(f32) + moved.astype(f32)).astype(bf16)


def halve(parts, axis):
    high = lax.axis_index(axis) // 2
    keep = lax.dynamic_slice_in_dim(parts, 2 * high, 2, 0)
    send = lax.dynamic_slice_in_dim(parts, 2 - 2 * high, 2, 0)
    return join(keep, meet(send, axis, 2))


def halve_again(two, axis):
    low = lax.rem(lax.axis_index(axis), 2)
    keep = lax.dynamic_index_in_dim(two, low, 0, keepdims=False)
    send = lax.dynamic_index_in_dim(two, 1 - low, 0, keepdims=False)
    return join(keep, meet(send, axis, 1))


def together(*arrays):
    return lax.optimization_barrier(arrays)


def outer(left, right):
    return lax.dot_general(left, right, (((0,), (0,)), ((), ())), preferred_element_type=f32)


def rows_by_rows(left, right):
    return lax.dot_general(left, right, (((1,), (1,)), ((), ())), preferred_element_type=f32)


def attend(lengths, qa, kv):
    heads = [(z, c) for z in range(4) for c in range(2)]
    q = jnp.concatenate([qa[z, :, c * HD : c * HD + HD] for z, c in heads], 0)
    g = jnp.concatenate([qa[z, :, 256 + c * HD : 256 + c * HD + HD] for z, c in heads], 0)
    token = lax.broadcasted_iota(jnp.int32, (1, 512), 1)
    limit = jnp.full((1, 512), lengths[3], jnp.int32)
    for y in range(2, -1, -1):
        limit = jnp.where(token < PT * (y + 1), lengths[y], limit)
    valid = (token & (PT - 1)) < limit
    scores = rows_by_rows(q, kv[:, :HD]) * SCALE
    weights = jnp.where(valid, jnp.exp(scores), 0.0)
    return q, g, weights, rows_by_rows(g, kv[:, HD:])


def projection_kernel(core, even, odd, own, other, out):
    at_first = core[0] == 0
    for i, at in enumerate((0, 512)):
        kept = jnp.where(at_first, even[i], odd[i])
        rest = jnp.where(at_first, odd[i], even[i])
        total = jnp.dot(kept, own[:, at : at + 256], preferred_element_type=f32)
        total = total + jnp.dot(rest, other[:, at : at + 256], preferred_element_type=f32)
        out[:, 256 * i : 256 * i + 256] = total.astype(bf16)


def forward_kernel(lengths, qa, kv, out):
    _, _, weights, dprob = attend(lengths, qa, kv)
    total = jnp.sum(weights, -1, keepdims=True)
    probs = weights / jnp.where(total > 0, total, 1.0)
    delta = jnp.sum(probs * dprob, -1, keepdims=True)
    centred = (probs * (dprob - delta)).astype(bf16)
    plain = jnp.dot(probs.astype(bf16), kv[...], preferred_element_type=f32).astype(bf16)
    slope = jnp.dot(centred, kv[:, :HD], preferred_element_type=f32).astype(bf16)
    lane = lax.broadcasted_iota(jnp.int32, (64, 128), 1)
    stats = jnp.zeros((64, 128), f32)
    columns = []
    for h in range(8):
        rows = slice(64 * h, 64 * h + 64)
        for value in (total[rows], delta[rows]):
            high = value.astype(bf16).astype(f32)
            columns += [high, value - high]
    for k, column in enumerate(columns):
        stats = jnp.where(lane == k, column, stats)
    for z in range(4):
        own = stats
        for k in range(8):
            own = jnp.where(lane == 32 + k, columns[8 * z + k], own)
        for c in range(2):
            rows = slice(128 * z + 64 * c, 128 * z + 64 * c + 64)
            out[z, :, c * HD : c * HD + HD] = slope[rows]
            out[z, :, 256 + c * HD : 256 + c * HD + HD] = plain[rows, :HD]
            out[z, :, 512 + c * HD : 512 + c * HD + HD] = plain[rows, HD:]
        out[z, :, 768:] = own.astype(bf16)


def combine(stats, k):
    totals = [s[:, k : k + 1] + s[:, k + 1 : k + 2] for s in stats]
    deltas = [s[:, k + 2 : k + 3] + s[:, k + 3 : k + 4] for s in stats]
    total = totals[0] + totals[1] + totals[2] + totals[3]
    shares = [t / total for t in totals]
    delta = sum(share * d for share, d in zip(shares, deltas))
    return total, delta, shares, deltas


def backward_kernel(lengths, moved, qa, kv, heads, kv_part):
    stats = [moved[i, :, 768:].astype(f32) for i in range(4)]
    for c in range(2):
        _, delta, shares, deltas = combine(stats, 32 + 4 * c)
        mixed = jnp.zeros((64, HD), f32)
        grad = jnp.zeros((64, HD), f32)
        for i in range(4):
            slope, key_mean, value_mean = (
                moved[i, :, at + c * HD : at + c * HD + HD].astype(f32) for at in (0, 256, 512)
            )
            mixed = mixed + shares[i] * value_mean
            grad = grad + shares[i] * (slope + (deltas[i] - delta) * key_mean)
        heads[:64, c * HD : c * HD + HD] = mixed.astype(bf16)
        heads[64:, c * HD : c * HD + HD] = (grad * SCALE).astype(bf16)
    pairs = [combine(stats, 4 * h)[:2] for h in range(8)]
    total = jnp.concatenate([pair[0] for pair in pairs], 0)
    delta = jnp.concatenate([pair[1] for pair in pairs], 0)
    q, g, weights, dprob = attend(lengths, qa, kv)
    probs = weights / total
    dscore = (probs * (dprob - delta) * SCALE).astype(bf16)
    key_part = outer(dscore, q).astype(bf16)
    value_part = outer(probs.astype(bf16), g).astype(bf16)
    kv_part[:, :HD] = key_part
    kv_part[:, HD:] = value_part


def key_term_kernel(core, kv_part, enc, keep, send):
    term = outer(enc[...], kv_part[...]).astype(bf16).reshape(16, 2, 64, 256)
    at_first = core[0] == 0
    keep[...] = jnp.where(at_first, term[:, 0], term[:, 1])
    send[...] = jnp.where(at_first, term[:, 1], term[:, 0])


def head_term_kernel(sources, moved, own, second, third, fourth, keep, send, kv_sum):
    q_term = o_term = jnp.zeros((512, 256), f32)
    kv_total = jnp.zeros((256, 256), f32)
    for step, rows in enumerate((own, second, third, fourth)):
        block = moved[sources[1 + step]]
        o_term = o_term + outer(rows[:, 512:], block[:64])
        q_term = q_term + outer(rows[:, :512], block[64:128])
        kv_total = kv_total + block[128:].astype(f32)
    term = jnp.concatenate([q_term, o_term], 1).astype(bf16)
    at_first = sources[0] == 0
    keep[...] = jnp.where(at_first, term[:256], term[256:])
    send[...] = jnp.where(at_first, term[256:], term[:256])
    kv_sum[...] = kv_total.astype(bf16)


def place_kernel(core, mine, theirs, q_out, o_out):
    at_first = core[0] == 0
    for half in range(2):
        block = jnp.where(at_first == (half == 0), mine[0], theirs[0])
        q_out[256 * half : 256 * half + 256, :] = block[:, :256].astype(f32)
        o_out[:, 256 * half : 256 * half + 256] = block[:, 256:].T


PARAMS = pltpu.CompilerParams(vmem_limit_bytes=16 * 1024 * 1024)
SCALARS = pl.BlockSpec(memory_space=pltpu.SMEM)


def call(kernel, outs, scalars, *arrays):
    vmem = pl.BlockSpec(memory_space=pltpu.VMEM)
    return pl.pallas_call(
        kernel,
        out_shape=[jax.ShapeDtypeStruct(shape, bf16) for shape in outs],
        in_specs=[SCALARS] + [vmem] * len(arrays),
        out_specs=[vmem] * len(outs),
        compiler_params=PARAMS,
    )(scalars, *arrays)


def place(core, mine, theirs):
    block = pl.BlockSpec((1, 256, 512), lambda i: (i, 0, 0))
    return pl.pallas_call(
        place_kernel,
        grid=(4,),
        out_shape=[
            jax.ShapeDtypeStruct((2048, 256), f32),
            jax.ShapeDtypeStruct((256, 2048), bf16),
        ],
        in_specs=[SCALARS, block, block],
        out_specs=[
            pl.BlockSpec((512, 256), lambda i: (i, 0)),
            pl.BlockSpec((256, 512), lambda i: (0, i)),
        ],
        compiler_params=PARAMS,
    )(core, mine, theirs)


def local(dec_states, enc_states, passage_lengths, q_weight, kv_weight, o_weight, out_grad):
    dec_rows = dec_states[0]
    enc_rows = enc_states[0]
    grad_rows = out_grad[0]
    core = lax.axis_index("co").astype(jnp.int32).reshape(1)
    first_core = lax.axis_index("co") == 0
    zl = lax.axis_index("zl")
    lengths = lax.dynamic_index_in_dim(passage_lengths[0].reshape(4, 4), zl, 1, keepdims=False)

    enc_four = spread(enc_rows, "y").reshape(512, 2048)

    shard = jnp.concatenate([q_weight, kv_weight, o_weight.T], 1)
    own = lax.all_gather(shard, "zh", axis=0, tiled=True)
    own, enc_four, dec_rows, grad_rows = together(own, enc_four, dec_rows, grad_rows)
    own = spread(own, "x").reshape(1024, 768)
    halves = jnp.stack([dec_rows, grad_rows]).reshape(2, 64, 16, 2, 64)
    even, odd = halves[:, :, :, 0].reshape(2, 64, 1024), halves[:, :, :, 1].reshape(2, 64, 1024)
    own, even, odd = together(own, even, odd)
    other = swap(own)
    (qa_own,) = call(projection_kernel, [(64, 512)], core, even, odd, own, other)
    own, other, qa_own = together(own, other, qa_own)
    own, other = own.reshape(16, 64, 768), other.reshape(16, 64, 768)
    weights_all = jnp.stack(
        [jnp.where(first_core, own, other), jnp.where(first_core, other, own)], 1
    ).reshape(2048, 768)
    wq_full = weights_all[:, :256]
    wkv_full = weights_all[:, 256:512]
    qa_all = spread(qa_own, "zl")
    kv_all = jnp.dot(enc_four, wkv_full, preferred_element_type=f32).astype(bf16)
    (parts,) = call(forward_kernel, [(4, 64, 896)], lengths, qa_all, kv_all)

    quarters = jnp.stack(
        [
            jnp.concatenate([dec_rows[:, at : at + 512], grad_rows[:, at : at + 512]], 1)
            for at in range(0, 2048, 512)
        ]
    )
    parts, quarters = together(parts, quarters)
    moved = lax.all_to_all(parts, "zl", 0, 0)
    x = lax.axis_index("x")
    rows_x = [lax.dynamic_index_in_dim(quarters, x, 0, keepdims=False)]
    for step in range(1, 4):
        part = lax.dynamic_index_in_dim(quarters, lax.rem(x + step, 4), 0, keepdims=False)
        rows_x.append(lax.ppermute(part, "x", [(i, (i + step) % 4) for i in range(4)]))
    moved, *rows_x = together(moved, *rows_x)
    heads, kv_part = call(backward_kernel, [(128, 256), (512, 256)], lengths, moved, qa_all, kv_all)

    keep, send = call(key_term_kernel, [(16, 64, 256)] * 2, core, kv_part, enc_four)
    kv_chip = join(keep, swap(send)).reshape(4, 256, 256)
    messages = jnp.concatenate([jnp.broadcast_to(heads[None], (4, 128, 256)), kv_chip], 1)
    messages, kv_part = together(messages, kv_part)
    moved_x = lax.all_to_all(messages, "x", 0, 0)
    kv_two = halve(kv_part.reshape(4, PT, 256), "y")
    moved_x, kv_two = together(moved_x, kv_two)
    sources = jnp.concatenate([core] + [lax.rem(x + 4 - step, 4).reshape(1) for step in range(4)])
    keep, send, kv_sum = call(
        head_term_kernel, [(256, 512), (256, 512), (256, 256)], sources, moved_x, *rows_x
    )
    sum_x = jnp.concatenate([join(keep, swap(send)), kv_sum], 1)
    sum_x, kv_two, heads = together(sum_x, kv_two, heads)

    sum_z = exchange(sum_x.reshape(4, 64, 768), "zh")
    kv_grad = halve_again(kv_two, "y")
    enc_grad = jnp.dot(kv_grad, wkv_full.T, preferred_element_type=f32).astype(bf16)
    dec_part = jnp.dot(heads[64:], wq_full.T, preferred_element_type=f32).astype(bf16)
    dec_part = dec_part.reshape(64, 4, 512).transpose(1, 0, 2)
    sum_z, dec_part, enc_grad = together(sum_z, dec_part, enc_grad)

    last = jnp.concatenate([jnp.broadcast_to(sum_z[None, :, 512:], (4, 64, 256)), dec_part], 2)
    last = exchange(last, "y")
    mine = lax.all_gather(sum_z[:, :512], "zh", axis=0, tiled=True)
    copies = jnp.broadcast_to(mine[None], (4, 256, 512))
    copies, last = together(copies, last)
    mine = lax.all_to_all(copies, "x", 0, 0)
    high, low = zl // 2, lax.rem(zl, 2)
    parts = last[:, 256:].reshape(64, 2, 256)
    ahead = lax.dynamic_index_in_dim(parts, 1 - high, 1, keepdims=False)
    back = meet(jnp.concatenate([last[:, :256], ahead], 1), "zl", 2)
    here = lax.dynamic_index_in_dim(parts, high, 1, keepdims=False)
    last = join(jnp.concatenate([last[:, :256], here], 1), back)
    mine, last = together(mine, last)
    parts = last[:, 256:].reshape(64, 2, 128)
    ahead = lax.dynamic_index_in_dim(parts, 1 - low, 1, keepdims=False)
    back = meet(jnp.concatenate([last[:, :256], ahead], 1), "zl", 1).astype(f32)
    here = lax.dynamic_index_in_dim(parts, low, 1, keepdims=False)
    kv_weight_grad = last[:, :256].astype(f32) + back[:, :256]
    dec_grad = (here.astype(f32) + back[:, 256:]).astype(bf16)
    q_weight_grad, o_weight_grad = place(core, mine, swap(mine))
    return (dec_grad[None], enc_grad[None], q_weight_grad, kv_weight_grad, o_weight_grad)


def solution(mesh):
    fine = Mesh(mesh.devices.reshape(4, 4, 2, 4, 4), ("x", "zh", "co", "y", "zl"))
    pb = ("x", "zh", "co")
    row = ("y", "zl")
    placed = (
        P(pb, None, None),
        P(pb, row, None),
        P(pb, None),
        P(pb, row),
        P(pb, None),
        P(row, pb),
        P(pb, None, None),
    )
    return jax.shard_map(
        local,
        mesh=fine,
        in_specs=placed,
        out_specs=(
            P(pb, None, row),
            P(pb, row, None),
            P(None, row),
            P(pb, None),
            P(row, None),
        ),
        check_vma=False,
    )
```

```python
import jax
import jax.numpy as jnp
from jax import lax
from jax.experimental import pallas as pl
from jax.experimental.pallas import tpu as pltpu
from jax.sharding import Mesh, PartitionSpec as P

HD = 128
PT = 128
SCALE = HD ** (-0.5)
f32 = jnp.float32
bf16 = jnp.bfloat16


def spread(block, axis):
    copies = jnp.broadcast_to(block[None], (4,) + block.shape)
    return lax.all_to_all(copies, axis, 0, 0)


def exchange(parts, axis):
    return jnp.sum(lax.all_to_all(parts, axis, 0, 0).astype(f32), 0).astype(bf16)


def swap(block):
    return lax.ppermute(block, "co", [(0, 1), (1, 0)])


def meet(block, axis, bit):
    return lax.ppermute(block, axis, [(i, i ^ bit) for i in range(4)])


def join(keep, moved):
    return (keep.astype(f32) + moved.astype(f32)).astype(bf16)


def halve(parts, axis):
    high = lax.axis_index(axis) // 2
    keep = lax.dynamic_slice_in_dim(parts, 2 * high, 2, 0)
    send = lax.dynamic_slice_in_dim(parts, 2 - 2 * high, 2, 0)
    return join(keep, meet(send, axis, 2))


def halve_again(two, axis):
    low = lax.rem(lax.axis_index(axis), 2)
    keep = lax.dynamic_index_in_dim(two, low, 0, keepdims=False)
    send = lax.dynamic_index_in_dim(two, 1 - low, 0, keepdims=False)
    return join(keep, meet(send, axis, 1))


def together(*arrays):
    return lax.optimization_barrier(arrays)


def outer(left, right):
    return lax.dot_general(left, right, (((0,), (0,)), ((), ())), preferred_element_type=f32)


def rows_by_rows(left, right):
    return lax.dot_general(left, right, (((1,), (1,)), ((), ())), preferred_element_type=f32)


def attend(lengths, qa, kv):
    heads = [(z, c) for z in range(4) for c in range(2)]
    q = jnp.concatenate([qa[z, :, c * HD : c * HD + HD] for z, c in heads], 0)
    g = jnp.concatenate([qa[z, :, 256 + c * HD : 256 + c * HD + HD] for z, c in heads], 0)
    token = lax.broadcasted_iota(jnp.int32, (1, 512), 1)
    limit = jnp.full((1, 512), lengths[3], jnp.int32)
    for y in range(2, -1, -1):
        limit = jnp.where(token < PT * (y + 1), lengths[y], limit)
    valid = (token & (PT - 1)) < limit
    scores = rows_by_rows(q, kv[:, :HD]) * SCALE
    weights = jnp.where(valid, jnp.exp(scores), 0.0)
    return q, g, weights, rows_by_rows(g, kv[:, HD:])


def projection_kernel(core, even, odd, own, other, out):
    at_first = core[0] == 0
    for i, at in enumerate((0, 512)):
        kept = jnp.where(at_first, even[i], odd[i])
        rest = jnp.where(at_first, odd[i], even[i])
        total = jnp.dot(kept, own[:, at : at + 256], preferred_element_type=f32)
        total = total + jnp.dot(rest, other[:, at : at + 256], preferred_element_type=f32)
        out[:, 256 * i : 256 * i + 256] = total.astype(bf16)


def forward_kernel(lengths, qa, kv, out):
    _, _, weights, dprob = attend(lengths, qa, kv)
    total = jnp.sum(weights, -1, keepdims=True)
    probs = weights / jnp.where(total > 0, total, 1.0)
    delta = jnp.sum(probs * dprob, -1, keepdims=True)
    centred = (probs * (dprob - delta)).astype(bf16)
    plain = jnp.dot(probs.astype(bf16), kv[...], preferred_element_type=f32).astype(bf16)
    slope = jnp.dot(centred, kv[:, :HD], preferred_element_type=f32).astype(bf16)
    lane = lax.broadcasted_iota(jnp.int32, (64, 128), 1)
    stats = jnp.zeros((64, 128), f32)
    columns = []
    for h in range(8):
        rows = slice(64 * h, 64 * h + 64)
        for value in (total[rows], delta[rows]):
            high = value.astype(bf16).astype(f32)
            columns += [high, value - high]
    for k, column in enumerate(columns):
        stats = jnp.where(lane == k, column, stats)
    for z in range(4):
        own = stats
        for k in range(8):
            own = jnp.where(lane == 32 + k, columns[8 * z + k], own)
        for c in range(2):
            rows = slice(128 * z + 64 * c, 128 * z + 64 * c + 64)
            out[z, :, c * HD : c * HD + HD] = slope[rows]
            out[z, :, 256 + c * HD : 256 + c * HD + HD] = plain[rows, :HD]
            out[z, :, 512 + c * HD : 512 + c * HD + HD] = plain[rows, HD:]
        out[z, :, 768:] = own.astype(bf16)


def combine(stats, k):
    totals = [s[:, k : k + 1] + s[:, k + 1 : k + 2] for s in stats]
    deltas = [s[:, k + 2 : k + 3] + s[:, k + 3 : k + 4] for s in stats]
    total = totals[0] + totals[1] + totals[2] + totals[3]
    shares = [t / total for t in totals]
    delta = sum(share * d for share, d in zip(shares, deltas))
    return total, delta, shares, deltas


def backward_kernel(lengths, moved, qa, kv, heads, kv_part):
    stats = [moved[i, :, 768:].astype(f32) for i in range(4)]
    for c in range(2):
        _, delta, shares, deltas = combine(stats, 32 + 4 * c)
        mixed = jnp.zeros((64, HD), f32)
        grad = jnp.zeros((64, HD), f32)
        for i in range(4):
            slope, key_mean, value_mean = (
                moved[i, :, at + c * HD : at + c * HD + HD].astype(f32) for at in (0, 256, 512)
            )
            mixed = mixed + shares[i] * value_mean
            grad = grad + shares[i] * (slope + (deltas[i] - delta) * key_mean)
        heads[:64, c * HD : c * HD + HD] = mixed.astype(bf16)
        heads[64:, c * HD : c * HD + HD] = (grad * SCALE).astype(bf16)
    pairs = [combine(stats, 4 * h)[:2] for h in range(8)]
    total = jnp.concatenate([pair[0] for pair in pairs], 0)
    delta = jnp.concatenate([pair[1] for pair in pairs], 0)
    q, g, weights, dprob = attend(lengths, qa, kv)
    probs = weights / total
    dscore = (probs * (dprob - delta) * SCALE).astype(bf16)
    key_part = outer(dscore, q).astype(bf16)
    value_part = outer(probs.astype(bf16), g).astype(bf16)
    kv_part[:, :HD] = key_part
    kv_part[:, HD:] = value_part


def key_term_kernel(core, kv_part, enc, keep, send):
    term = outer(enc[...], kv_part[...]).astype(bf16).reshape(16, 2, 64, 256)
    at_first = core[0] == 0
    keep[...] = jnp.where(at_first, term[:, 0], term[:, 1])
    send[...] = jnp.where(at_first, term[:, 1], term[:, 0])


def head_term_kernel(sources, moved, own, second, third, fourth, keep, send, kv_sum):
    q_term = o_term = jnp.zeros((512, 256), f32)
    kv_total = jnp.zeros((256, 256), f32)
    for step, rows in enumerate((own, second, third, fourth)):
        block = moved[sources[1 + step]]
        o_term = o_term + outer(rows[:, 512:], block[:64])
        q_term = q_term + outer(rows[:, :512], block[64:128])
        kv_total = kv_total + block[128:].astype(f32)
    term = jnp.concatenate([q_term, o_term], 1).astype(bf16)
    at_first = sources[0] == 0
    keep[...] = jnp.where(at_first, term[:256], term[256:])
    send[...] = jnp.where(at_first, term[256:], term[:256])
    kv_sum[...] = kv_total.astype(bf16)


def place_kernel(core, mine, theirs, q_out, o_out):
    at_first = core[0] == 0
    for half in range(2):
        block = jnp.where(at_first == (half == 0), mine[0], theirs[0])
        q_out[256 * half : 256 * half + 256, :] = block[:, :256].astype(f32)
        o_out[:, 256 * half : 256 * half + 256] = block[:, 256:].T


PARAMS = pltpu.CompilerParams(vmem_limit_bytes=16 * 1024 * 1024)
SCALARS = pl.BlockSpec(memory_space=pltpu.SMEM)


def call(kernel, outs, scalars, *arrays):
    vmem = pl.BlockSpec(memory_space=pltpu.VMEM)
    return pl.pallas_call(
        kernel,
        out_shape=[jax.ShapeDtypeStruct(shape, bf16) for shape in outs],
        in_specs=[SCALARS] + [vmem] * len(arrays),
        out_specs=[vmem] * len(outs),
        compiler_params=PARAMS,
    )(scalars, *arrays)


def place(core, mine, theirs):
    block = pl.BlockSpec((1, 256, 512), lambda i: (i, 0, 0))
    return pl.pallas_call(
        place_kernel,
        grid=(4,),
        out_shape=[
            jax.ShapeDtypeStruct((2048, 256), f32),
            jax.ShapeDtypeStruct((256, 2048), bf16),
        ],
        in_specs=[SCALARS, block, block],
        out_specs=[
            pl.BlockSpec((512, 256), lambda i: (i, 0)),
            pl.BlockSpec((256, 512), lambda i: (0, i)),
        ],
        compiler_params=PARAMS,
    )(core, mine, theirs)


def local(dec_states, enc_states, passage_lengths, q_weight, kv_weight, o_weight, out_grad):
    dec_rows = dec_states[0]
    enc_rows = enc_states[0]
    grad_rows = out_grad[0]
    core = lax.axis_index("co").astype(jnp.int32).reshape(1)
    first_core = lax.axis_index("co") == 0
    zl = lax.axis_index("zl")
    lengths = lax.dynamic_index_in_dim(passage_lengths[0].reshape(4, 4), zl, 1, keepdims=False)

    enc_four = spread(enc_rows, "y").reshape(512, 2048)

    shard = jnp.concatenate([q_weight, kv_weight, o_weight.T], 1)
    own = lax.all_gather(shard, "zh", axis=0, tiled=True)
    own, enc_four, dec_rows, grad_rows = together(own, enc_four, dec_rows, grad_rows)
    own = spread(own, "x").reshape(1024, 768)
    halves = jnp.stack([dec_rows, grad_rows]).reshape(2, 64, 16, 2, 64)
    even, odd = halves[:, :, :, 0].reshape(2, 64, 1024), halves[:, :, :, 1].reshape(2, 64, 1024)
    own, even, odd = together(own, even, odd)
    other = swap(own)
    (qa_own,) = call(projection_kernel, [(64, 512)], core, even, odd, own, other)
    own, other, qa_own = together(own, other, qa_own)
    own, other = own.reshape(16, 64, 768), other.reshape(16, 64, 768)
    weights_all = jnp.stack(
        [jnp.where(first_core, own, other), jnp.where(first_core, other, own)], 1
    ).reshape(2048, 768)
    wq_full = weights_all[:, :256]
    wkv_full = weights_all[:, 256:512]
    qa_all = spread(qa_own, "zl")
    kv_all = jnp.dot(enc_four, wkv_full, preferred_element_type=f32).astype(bf16)
    (parts,) = call(forward_kernel, [(4, 64, 896)], lengths, qa_all, kv_all)

    quarters = jnp.stack(
        [
            jnp.concatenate([dec_rows[:, at : at + 512], grad_rows[:, at : at + 512]], 1)
            for at in range(0, 2048, 512)
        ]
    )
    parts, quarters = together(parts, quarters)
    moved = lax.all_to_all(parts, "zl", 0, 0)
    x = lax.axis_index("x")
    rows_x = [lax.dynamic_index_in_dim(quarters, x, 0, keepdims=False)]
    for step in range(1, 4):
        part = lax.dynamic_index_in_dim(quarters, lax.rem(x + step, 4), 0, keepdims=False)
        rows_x.append(lax.ppermute(part, "x", [(i, (i + step) % 4) for i in range(4)]))
    moved, *rows_x = together(moved, *rows_x)
    heads, kv_part = call(backward_kernel, [(128, 256), (512, 256)], lengths, moved, qa_all, kv_all)

    keep, send = call(key_term_kernel, [(16, 64, 256)] * 2, core, kv_part, enc_four)
    kv_chip = join(keep, swap(send)).reshape(4, 256, 256)
    messages = jnp.concatenate([jnp.broadcast_to(heads[None], (4, 128, 256)), kv_chip], 1)
    messages, heads = together(messages, heads)
    moved_x = lax.all_to_all(messages, "x", 0, 0)
    dec_part = jnp.dot(heads[64:], wq_full.T, preferred_element_type=f32).astype(bf16)
    dec_two = halve(dec_part.reshape(64, 4, 4, 128).transpose(2, 0, 1, 3).reshape(4, 64, 512), "zl")
    moved_x, dec_two = together(moved_x, dec_two)
    sources = jnp.concatenate([core] + [lax.rem(x + 4 - step, 4).reshape(1) for step in range(4)])
    keep, send, kv_sum = call(
        head_term_kernel, [(256, 512), (256, 512), (256, 256)], sources, moved_x, *rows_x
    )
    sum_x = jnp.concatenate([join(keep, swap(send)), kv_sum], 1)
    sum_x, kv_part, dec_two = together(sum_x, kv_part, dec_two)

    sum_z = exchange(sum_x.reshape(4, 64, 768), "zh")
    rest = [
        halve_again(dec_two, "zl").reshape(64, 4, 128).transpose(1, 0, 2),
        kv_part.reshape(4, 2, 64, 256).transpose(0, 2, 1, 3).reshape(4, 64, 512),
    ]
    sum_z, *rest = together(sum_z, *rest)

    last = jnp.concatenate([jnp.broadcast_to(sum_z[None, :, 512:], (4, 64, 256)), *rest], 2)
    last = exchange(last, "y")
    mine = lax.all_gather(sum_z[:, :512], "zh", axis=0, tiled=True)
    copies = jnp.broadcast_to(mine[None], (4, 256, 512))
    copies, last = together(copies, last)
    mine = lax.all_to_all(copies, "x", 0, 0)
    dec_grad = last[:, 256:384]
    kv_grad = jnp.concatenate([last[:, 384:640], last[:, 640:]], 0)
    enc_grad = jnp.dot(kv_grad, wkv_full.T, preferred_element_type=f32).astype(bf16)
    kv_weight_grad = jnp.sum(lax.all_gather(last[:, :256], "zl", axis=0).astype(f32), 0)
    mine, kv_weight_grad, enc_grad = together(mine, kv_weight_grad, enc_grad)
    q_weight_grad, o_weight_grad = place(core, mine, swap(mine))
    return (dec_grad[None], enc_grad[None], q_weight_grad, kv_weight_grad, o_weight_grad)


def solution(mesh):
    fine = Mesh(mesh.devices.reshape(4, 4, 2, 4, 4), ("x", "zh", "co", "y", "zl"))
    pb = ("x", "zh", "co")
    row = ("y", "zl")
    placed = (
        P(pb, None, None),
        P(pb, row, None),
        P(pb, None),
        P(pb, row),
        P(pb, None),
        P(row, pb),
        P(pb, None, None),
    )
    return jax.shard_map(
        local,
        mesh=fine,
        in_specs=placed,
        out_specs=(
            P(pb, None, row),
            P(pb, row, None),
            P(None, row),
            P(pb, None),
            P(row, None),
        ),
        check_vma=False,
    )
```

```python
import jax
import jax.numpy as jnp
from jax import lax
from jax.experimental import pallas as pl
from jax.experimental.pallas import tpu as pltpu
from jax.sharding import Mesh, PartitionSpec as P

HD = 128
PT = 128
SCALE = HD ** (-0.5)
f32 = jnp.float32
bf16 = jnp.bfloat16


def spread(block, axis):
    copies = jnp.broadcast_to(block[None], (4,) + block.shape)
    return lax.all_to_all(copies, axis, 0, 0)


def exchange(parts, axis):
    return jnp.sum(lax.all_to_all(parts, axis, 0, 0).astype(f32), 0).astype(bf16)


def swap(block):
    return lax.ppermute(block, "co", [(0, 1), (1, 0)])


def meet(block, axis, bit):
    return lax.ppermute(block, axis, [(i, i ^ bit) for i in range(4)])


def join(keep, moved):
    return (keep.astype(f32) + moved.astype(f32)).astype(bf16)


def halve(parts, axis):
    high = lax.axis_index(axis) // 2
    keep = lax.dynamic_slice_in_dim(parts, 2 * high, 2, 0)
    send = lax.dynamic_slice_in_dim(parts, 2 - 2 * high, 2, 0)
    return join(keep, meet(send, axis, 2))


def halve_again(two, axis):
    low = lax.rem(lax.axis_index(axis), 2)
    keep = lax.dynamic_index_in_dim(two, low, 0, keepdims=False)
    send = lax.dynamic_index_in_dim(two, 1 - low, 0, keepdims=False)
    return join(keep, meet(send, axis, 1))


def together(*arrays):
    return lax.optimization_barrier(arrays)


def outer(left, right):
    return lax.dot_general(left, right, (((0,), (0,)), ((), ())), preferred_element_type=f32)


def rows_by_rows(left, right):
    return lax.dot_general(left, right, (((1,), (1,)), ((), ())), preferred_element_type=f32)


def attend(lengths, qa, kv):
    heads = [(z, c) for z in range(4) for c in range(2)]
    q = jnp.concatenate([qa[z, :, c * HD : c * HD + HD] for z, c in heads], 0)
    g = jnp.concatenate([qa[z, :, 256 + c * HD : 256 + c * HD + HD] for z, c in heads], 0)
    token = lax.broadcasted_iota(jnp.int32, (1, 512), 1)
    limit = jnp.full((1, 512), lengths[3], jnp.int32)
    for y in range(2, -1, -1):
        limit = jnp.where(token < PT * (y + 1), lengths[y], limit)
    valid = (token & (PT - 1)) < limit
    scores = rows_by_rows(q, kv[:, :HD]) * SCALE
    weights = jnp.where(valid, jnp.exp(scores), 0.0)
    return q, g, weights, rows_by_rows(g, kv[:, HD:])


def projection_kernel(core, even, odd, own, other, out):
    at_first = core[0] == 0
    for i, at in enumerate((0, 512)):
        kept = jnp.where(at_first, even[i], odd[i])
        rest = jnp.where(at_first, odd[i], even[i])
        total = jnp.dot(kept, own[:, at : at + 256], preferred_element_type=f32)
        total = total + jnp.dot(rest, other[:, at : at + 256], preferred_element_type=f32)
        out[:, 256 * i : 256 * i + 256] = total.astype(bf16)


def forward_kernel(lengths, qa, kv, out):
    _, _, weights, dprob = attend(lengths, qa, kv)
    total = jnp.sum(weights, -1, keepdims=True)
    probs = weights / jnp.where(total > 0, total, 1.0)
    delta = jnp.sum(probs * dprob, -1, keepdims=True)
    centred = (probs * (dprob - delta)).astype(bf16)
    plain = jnp.dot(probs.astype(bf16), kv[...], preferred_element_type=f32).astype(bf16)
    slope = jnp.dot(centred, kv[:, :HD], preferred_element_type=f32).astype(bf16)
    lane = lax.broadcasted_iota(jnp.int32, (64, 128), 1)
    stats = jnp.zeros((64, 128), f32)
    columns = []
    for h in range(8):
        rows = slice(64 * h, 64 * h + 64)
        for value in (total[rows], delta[rows]):
            high = value.astype(bf16).astype(f32)
            columns += [high, value - high]
    for k, column in enumerate(columns):
        stats = jnp.where(lane == k, column, stats)
    for z in range(4):
        own = stats
        for k in range(8):
            own = jnp.where(lane == 32 + k, columns[8 * z + k], own)
        for c in range(2):
            rows = slice(128 * z + 64 * c, 128 * z + 64 * c + 64)
            out[z, :, c * HD : c * HD + HD] = slope[rows]
            out[z, :, 256 + c * HD : 256 + c * HD + HD] = plain[rows, :HD]
            out[z, :, 512 + c * HD : 512 + c * HD + HD] = plain[rows, HD:]
        out[z, :, 768:] = own.astype(bf16)


def combine(stats, k):
    totals = [s[:, k : k + 1] + s[:, k + 1 : k + 2] for s in stats]
    deltas = [s[:, k + 2 : k + 3] + s[:, k + 3 : k + 4] for s in stats]
    total = totals[0] + totals[1] + totals[2] + totals[3]
    shares = [t / total for t in totals]
    delta = sum(share * d for share, d in zip(shares, deltas))
    return total, delta, shares, deltas


def backward_kernel(lengths, moved, qa, kv, heads, kv_part):
    stats = [moved[i, :, 768:].astype(f32) for i in range(4)]
    for c in range(2):
        _, delta, shares, deltas = combine(stats, 32 + 4 * c)
        mixed = jnp.zeros((64, HD), f32)
        grad = jnp.zeros((64, HD), f32)
        for i in range(4):
            slope, key_mean, value_mean = (
                moved[i, :, at + c * HD : at + c * HD + HD].astype(f32) for at in (0, 256, 512)
            )
            mixed = mixed + shares[i] * value_mean
            grad = grad + shares[i] * (slope + (deltas[i] - delta) * key_mean)
        heads[:64, c * HD : c * HD + HD] = mixed.astype(bf16)
        heads[64:, c * HD : c * HD + HD] = (grad * SCALE).astype(bf16)
    pairs = [combine(stats, 4 * h)[:2] for h in range(8)]
    total = jnp.concatenate([pair[0] for pair in pairs], 0)
    delta = jnp.concatenate([pair[1] for pair in pairs], 0)
    q, g, weights, dprob = attend(lengths, qa, kv)
    probs = weights / total
    dscore = (probs * (dprob - delta) * SCALE).astype(bf16)
    key_part = outer(dscore, q).astype(bf16)
    value_part = outer(probs.astype(bf16), g).astype(bf16)
    kv_part[:, :HD] = key_part
    kv_part[:, HD:] = value_part


def key_term_kernel(core, kv_part, enc, keep, send):
    term = outer(enc[...], kv_part[...]).astype(bf16).reshape(16, 2, 64, 256)
    at_first = core[0] == 0
    keep[...] = jnp.where(at_first, term[:, 0], term[:, 1])
    send[...] = jnp.where(at_first, term[:, 1], term[:, 0])


def head_term_kernel(sources, moved, own, second, third, fourth, keep, send, kv_sum):
    q_term = o_term = jnp.zeros((512, 256), f32)
    kv_total = jnp.zeros((256, 256), f32)
    for step, rows in enumerate((own, second, third, fourth)):
        block = moved[sources[1 + step]]
        o_term = o_term + outer(rows[:, 512:], block[:64])
        q_term = q_term + outer(rows[:, :512], block[64:128])
        kv_total = kv_total + block[128:].astype(f32)
    term = jnp.concatenate([q_term, o_term], 1).astype(bf16)
    at_first = sources[0] == 0
    keep[...] = jnp.where(at_first, term[:256], term[256:])
    send[...] = jnp.where(at_first, term[256:], term[:256])
    kv_sum[...] = kv_total.astype(bf16)


def place_kernel(core, mine, theirs, q_out, o_out):
    at_first = core[0] == 0
    for half in range(2):
        block = jnp.where(at_first == (half == 0), mine[0], theirs[0])
        q_out[256 * half : 256 * half + 256, :] = block[:, :256].astype(f32)
        o_out[:, 256 * half : 256 * half + 256] = block[:, 256:].T


PARAMS = pltpu.CompilerParams(vmem_limit_bytes=16 * 1024 * 1024)
SCALARS = pl.BlockSpec(memory_space=pltpu.SMEM)


def call(kernel, outs, scalars, *arrays):
    vmem = pl.BlockSpec(memory_space=pltpu.VMEM)
    return pl.pallas_call(
        kernel,
        out_shape=[jax.ShapeDtypeStruct(shape, bf16) for shape in outs],
        in_specs=[SCALARS] + [vmem] * len(arrays),
        out_specs=[vmem] * len(outs),
        compiler_params=PARAMS,
    )(scalars, *arrays)


def place(core, mine, theirs):
    block = pl.BlockSpec((1, 256, 512), lambda i: (i, 0, 0))
    return pl.pallas_call(
        place_kernel,
        grid=(4,),
        out_shape=[
            jax.ShapeDtypeStruct((2048, 256), f32),
            jax.ShapeDtypeStruct((256, 2048), bf16),
        ],
        in_specs=[SCALARS, block, block],
        out_specs=[
            pl.BlockSpec((512, 256), lambda i: (i, 0)),
            pl.BlockSpec((256, 512), lambda i: (0, i)),
        ],
        compiler_params=PARAMS,
    )(core, mine, theirs)


def local(dec_states, enc_states, passage_lengths, q_weight, kv_weight, o_weight, out_grad):
    dec_rows = dec_states[0]
    enc_rows = enc_states[0]
    grad_rows = out_grad[0]
    core = lax.axis_index("co").astype(jnp.int32).reshape(1)
    first_core = lax.axis_index("co") == 0
    zl = lax.axis_index("zl")
    lengths = lax.dynamic_index_in_dim(passage_lengths[0].reshape(4, 4), zl, 1, keepdims=False)

    enc_four = spread(enc_rows, "y").reshape(512, 2048)

    shard = jnp.concatenate([q_weight, kv_weight, o_weight.T], 1)
    own = lax.all_gather(shard, "zh", axis=0, tiled=True)
    own, enc_four, dec_rows, grad_rows = together(own, enc_four, dec_rows, grad_rows)
    own = spread(own, "x").reshape(1024, 768)
    halves = jnp.stack([dec_rows, grad_rows]).reshape(2, 64, 16, 2, 64)
    even, odd = halves[:, :, :, 0].reshape(2, 64, 1024), halves[:, :, :, 1].reshape(2, 64, 1024)
    own, even, odd = together(own, even, odd)
    other = swap(own)
    (qa_own,) = call(projection_kernel, [(64, 512)], core, even, odd, own, other)
    own, other, qa_own = together(own, other, qa_own)
    own, other = own.reshape(16, 64, 768), other.reshape(16, 64, 768)
    weights_all = jnp.stack(
        [jnp.where(first_core, own, other), jnp.where(first_core, other, own)], 1
    ).reshape(2048, 768)
    wq_full = weights_all[:, :256]
    wkv_full = weights_all[:, 256:512]
    qa_all = spread(qa_own, "zl")
    kv_all = jnp.dot(enc_four, wkv_full, preferred_element_type=f32).astype(bf16)
    (parts,) = call(forward_kernel, [(4, 64, 896)], lengths, qa_all, kv_all)

    quarters = jnp.stack(
        [
            jnp.concatenate([dec_rows[:, at : at + 512], grad_rows[:, at : at + 512]], 1)
            for at in range(0, 2048, 512)
        ]
    )
    parts, quarters = together(parts, quarters)
    moved = lax.all_to_all(parts, "zl", 0, 0)
    x = lax.axis_index("x")
    rows_x = [lax.dynamic_index_in_dim(quarters, x, 0, keepdims=False)]
    for step in range(1, 4):
        part = lax.dynamic_index_in_dim(quarters, lax.rem(x + step, 4), 0, keepdims=False)
        rows_x.append(lax.ppermute(part, "x", [(i, (i + step) % 4) for i in range(4)]))
    moved, *rows_x = together(moved, *rows_x)
    heads, kv_part = call(backward_kernel, [(128, 256), (512, 256)], lengths, moved, qa_all, kv_all)

    keep, send = call(key_term_kernel, [(16, 64, 256)] * 2, core, kv_part, enc_four)
    kv_chip = join(keep, swap(send)).reshape(4, 256, 256)
    messages = jnp.concatenate([jnp.broadcast_to(heads[None], (4, 128, 256)), kv_chip], 1)
    messages, heads = together(messages, heads)
    moved_x = lax.all_to_all(messages, "x", 0, 0)
    dec_part = jnp.dot(heads[64:], wq_full.T, preferred_element_type=f32).astype(bf16)
    dec_two = halve(dec_part.reshape(64, 4, 4, 128).transpose(2, 0, 1, 3).reshape(4, 64, 512), "zl")
    dec_zl = halve_again(dec_two, "zl")
    moved_x, dec_zl = together(moved_x, dec_zl)
    sources = jnp.concatenate([core] + [lax.rem(x + 4 - step, 4).reshape(1) for step in range(4)])
    keep, send, kv_sum = call(
        head_term_kernel, [(256, 512), (256, 512), (256, 256)], sources, moved_x, *rows_x
    )
    sum_x = jnp.concatenate([join(keep, swap(send)), kv_sum], 1)
    sum_x, kv_part, dec_zl = together(sum_x, kv_part, dec_zl)

    sum_z = exchange(sum_x.reshape(4, 64, 768), "zh")
    rest = [
        dec_zl.reshape(64, 4, 128).transpose(1, 0, 2),
        kv_part.reshape(4, 2, 64, 256).transpose(0, 2, 1, 3).reshape(4, 64, 512),
    ]
    sum_z, *rest = together(sum_z, *rest)

    last = jnp.concatenate([jnp.broadcast_to(sum_z[None, :, 512:], (4, 64, 256)), *rest], 2)
    last = exchange(last, "y")
    mine = lax.all_gather(sum_z[:, :512], "zh", axis=0, tiled=True)
    copies = jnp.broadcast_to(mine[None], (4, 256, 512))
    copies, last = together(copies, last)
    mine = lax.all_to_all(copies, "x", 0, 0)
    dec_grad = last[:, 256:384]
    kv_grad = jnp.concatenate([last[:, 384:640], last[:, 640:]], 0)
    enc_grad = jnp.dot(kv_grad, wkv_full.T, preferred_element_type=f32).astype(bf16)
    kv_weight_grad = jnp.sum(lax.all_gather(last[:, :256], "zl", axis=0).astype(f32), 0)
    mine, kv_weight_grad, enc_grad = together(mine, kv_weight_grad, enc_grad)
    q_weight_grad, o_weight_grad = place(core, mine, swap(mine))
    return (dec_grad[None], enc_grad[None], q_weight_grad, kv_weight_grad, o_weight_grad)


def solution(mesh):
    fine = Mesh(mesh.devices.reshape(4, 4, 2, 4, 4), ("x", "zh", "co", "y", "zl"))
    pb = ("x", "zh", "co")
    row = ("y", "zl")
    placed = (
        P(pb, None, None),
        P(pb, row, None),
        P(pb, None),
        P(pb, row),
        P(pb, None),
        P(row, pb),
        P(pb, None, None),
    )
    return jax.shard_map(
        local,
        mesh=fine,
        in_specs=placed,
        out_specs=(
            P(pb, None, row),
            P(pb, row, None),
            P(None, row),
            P(pb, None),
            P(row, None),
        ),
        check_vma=False,
    )
```

```python
import jax
import jax.numpy as jnp
from jax import lax
from jax.experimental import pallas as pl
from jax.experimental.pallas import tpu as pltpu
from jax.sharding import Mesh, PartitionSpec as P

HD = 128
PT = 128
SCALE = HD ** (-0.5)
f32 = jnp.float32
bf16 = jnp.bfloat16


def spread(block, axis):
    copies = jnp.broadcast_to(block[None], (4,) + block.shape)
    return lax.all_to_all(copies, axis, 0, 0)


def exchange(parts, axis):
    return jnp.sum(lax.all_to_all(parts, axis, 0, 0).astype(f32), 0).astype(bf16)


def swap(block):
    return lax.ppermute(block, "co", [(0, 1), (1, 0)])


def meet(block, axis, bit):
    return lax.ppermute(block, axis, [(i, i ^ bit) for i in range(4)])


def join(keep, moved):
    return (keep.astype(f32) + moved.astype(f32)).astype(bf16)


def together(*arrays):
    return lax.optimization_barrier(arrays)


def outer(left, right):
    return lax.dot_general(left, right, (((0,), (0,)), ((), ())), preferred_element_type=f32)


def rows_by_rows(left, right):
    return lax.dot_general(left, right, (((1,), (1,)), ((), ())), preferred_element_type=f32)


def attend(lengths, qa, kv):
    heads = [(z, c) for z in range(4) for c in range(2)]
    q = jnp.concatenate([qa[z, :, c * HD : c * HD + HD] for z, c in heads], 0)
    g = jnp.concatenate([qa[z, :, 256 + c * HD : 256 + c * HD + HD] for z, c in heads], 0)
    token = lax.broadcasted_iota(jnp.int32, (1, 512), 1)
    limit = jnp.full((1, 512), lengths[3], jnp.int32)
    for y in range(2, -1, -1):
        limit = jnp.where(token < PT * (y + 1), lengths[y], limit)
    valid = (token & (PT - 1)) < limit
    scores = rows_by_rows(q, kv[:, :HD]) * SCALE
    weights = jnp.where(valid, jnp.exp(scores), 0.0)
    return q, g, weights, rows_by_rows(g, kv[:, HD:])


def projection_kernel(core, even, odd, own, other, out):
    at_first = core[0] == 0
    for i, at in enumerate((0, 512)):
        kept = jnp.where(at_first, even[i], odd[i])
        rest = jnp.where(at_first, odd[i], even[i])
        total = jnp.dot(kept, own[:, at : at + 256], preferred_element_type=f32)
        total = total + jnp.dot(rest, other[:, at : at + 256], preferred_element_type=f32)
        out[:, 256 * i : 256 * i + 256] = total.astype(bf16)


def forward_kernel(lengths, qa, kv, out):
    _, _, weights, dprob = attend(lengths, qa, kv)
    total = jnp.sum(weights, -1, keepdims=True)
    probs = weights / jnp.where(total > 0, total, 1.0)
    delta = jnp.sum(probs * dprob, -1, keepdims=True)
    centred = (probs * (dprob - delta)).astype(bf16)
    plain = jnp.dot(probs.astype(bf16), kv[...], preferred_element_type=f32).astype(bf16)
    slope = jnp.dot(centred, kv[:, :HD], preferred_element_type=f32).astype(bf16)
    lane = lax.broadcasted_iota(jnp.int32, (64, 128), 1)
    stats = jnp.zeros((64, 128), f32)
    columns = []
    for h in range(8):
        rows = slice(64 * h, 64 * h + 64)
        for value in (total[rows], delta[rows]):
            high = value.astype(bf16).astype(f32)
            columns += [high, value - high]
    for k, column in enumerate(columns):
        stats = jnp.where(lane == k, column, stats)
    for z in range(4):
        own = stats
        for k in range(8):
            own = jnp.where(lane == 32 + k, columns[8 * z + k], own)
        for c in range(2):
            rows = slice(128 * z + 64 * c, 128 * z + 64 * c + 64)
            out[z, :, c * HD : c * HD + HD] = slope[rows]
            out[z, :, 256 + c * HD : 256 + c * HD + HD] = plain[rows, :HD]
            out[z, :, 512 + c * HD : 512 + c * HD + HD] = plain[rows, HD:]
        out[z, :, 768:] = own.astype(bf16)


def combine(stats, k):
    totals = [s[:, k : k + 1] + s[:, k + 1 : k + 2] for s in stats]
    deltas = [s[:, k + 2 : k + 3] + s[:, k + 3 : k + 4] for s in stats]
    total = totals[0] + totals[1] + totals[2] + totals[3]
    shares = [t / total for t in totals]
    delta = sum(share * d for share, d in zip(shares, deltas))
    return total, delta, shares, deltas


def backward_kernel(lengths, moved, qa, kv, heads, kv_part):
    stats = [moved[i, :, 768:].astype(f32) for i in range(4)]
    for c in range(2):
        _, delta, shares, deltas = combine(stats, 32 + 4 * c)
        mixed = jnp.zeros((64, HD), f32)
        grad = jnp.zeros((64, HD), f32)
        for i in range(4):
            slope, key_mean, value_mean = (
                moved[i, :, at + c * HD : at + c * HD + HD].astype(f32) for at in (0, 256, 512)
            )
            mixed = mixed + shares[i] * value_mean
            grad = grad + shares[i] * (slope + (deltas[i] - delta) * key_mean)
        heads[:64, c * HD : c * HD + HD] = mixed.astype(bf16)
        heads[64:, c * HD : c * HD + HD] = (grad * SCALE).astype(bf16)
    pairs = [combine(stats, 4 * h)[:2] for h in range(8)]
    total = jnp.concatenate([pair[0] for pair in pairs], 0)
    delta = jnp.concatenate([pair[1] for pair in pairs], 0)
    q, g, weights, dprob = attend(lengths, qa, kv)
    probs = weights / total
    dscore = (probs * (dprob - delta) * SCALE).astype(bf16)
    key_part = outer(dscore, q).astype(bf16)
    value_part = outer(probs.astype(bf16), g).astype(bf16)
    kv_part[:, :HD] = key_part
    kv_part[:, HD:] = value_part


def key_term_kernel(core, kv_part, enc, keep, send):
    term = outer(enc[...], kv_part[...]).astype(bf16).reshape(16, 2, 64, 256)
    at_first = core[0] == 0
    keep[...] = jnp.where(at_first, term[:, 0], term[:, 1])
    send[...] = jnp.where(at_first, term[:, 1], term[:, 0])


def head_term_kernel(sources, moved, own, second, third, fourth, keep, send, kv_sum):
    q_term = o_term = jnp.zeros((512, 256), f32)
    kv_total = jnp.zeros((256, 256), f32)
    for step, rows in enumerate((own, second, third, fourth)):
        block = moved[sources[1 + step]]
        o_term = o_term + outer(rows[:, 512:], block[:64])
        q_term = q_term + outer(rows[:, :512], block[64:128])
        kv_total = kv_total + block[128:].astype(f32)
    term = jnp.concatenate([q_term, o_term], 1).astype(bf16)
    at_first = sources[0] == 0
    keep[...] = jnp.where(at_first, term[:256], term[256:])
    send[...] = jnp.where(at_first, term[256:], term[:256])
    kv_sum[...] = kv_total.astype(bf16)


def place_kernel(core, mine, theirs, q_out, o_out):
    at_first = core[0] == 0
    for half in range(2):
        block = jnp.where(at_first == (half == 0), mine[0], theirs[0])
        q_out[256 * half : 256 * half + 256, :] = block[:, :256].astype(f32)
        o_out[:, 256 * half : 256 * half + 256] = block[:, 256:].T


PARAMS = pltpu.CompilerParams(vmem_limit_bytes=16 * 1024 * 1024)
SCALARS = pl.BlockSpec(memory_space=pltpu.SMEM)


def call(kernel, outs, scalars, *arrays):
    vmem = pl.BlockSpec(memory_space=pltpu.VMEM)
    return pl.pallas_call(
        kernel,
        out_shape=[jax.ShapeDtypeStruct(shape, bf16) for shape in outs],
        in_specs=[SCALARS] + [vmem] * len(arrays),
        out_specs=[vmem] * len(outs),
        compiler_params=PARAMS,
    )(scalars, *arrays)


def place(core, mine, theirs):
    block = pl.BlockSpec((1, 256, 512), lambda i: (i, 0, 0))
    return pl.pallas_call(
        place_kernel,
        grid=(4,),
        out_shape=[
            jax.ShapeDtypeStruct((2048, 256), f32),
            jax.ShapeDtypeStruct((256, 2048), bf16),
        ],
        in_specs=[SCALARS, block, block],
        out_specs=[
            pl.BlockSpec((512, 256), lambda i: (i, 0)),
            pl.BlockSpec((256, 512), lambda i: (0, i)),
        ],
        compiler_params=PARAMS,
    )(core, mine, theirs)


def local(dec_states, enc_states, passage_lengths, q_weight, kv_weight, o_weight, out_grad):
    dec_rows = dec_states[0]
    enc_rows = enc_states[0]
    grad_rows = out_grad[0]
    core = lax.axis_index("co").astype(jnp.int32).reshape(1)
    first_core = lax.axis_index("co") == 0
    zl = lax.axis_index("zl")
    lengths = lax.dynamic_index_in_dim(passage_lengths[0].reshape(4, 4), zl, 1, keepdims=False)

    enc_four = spread(enc_rows, "y").reshape(512, 2048)

    shard = jnp.concatenate([q_weight, kv_weight, o_weight.T], 1)
    own = lax.all_gather(shard, "zh", axis=0, tiled=True)
    own, enc_four, dec_rows, grad_rows = together(own, enc_four, dec_rows, grad_rows)
    own = spread(own, "x").reshape(1024, 768)
    halves = jnp.stack([dec_rows, grad_rows]).reshape(2, 64, 16, 2, 64)
    even, odd = halves[:, :, :, 0].reshape(2, 64, 1024), halves[:, :, :, 1].reshape(2, 64, 1024)
    own, even, odd = together(own, even, odd)
    other = swap(own)
    (qa_own,) = call(projection_kernel, [(64, 512)], core, even, odd, own, other)
    own, other, qa_own = together(own, other, qa_own)
    own, other = own.reshape(16, 64, 768), other.reshape(16, 64, 768)
    weights_all = jnp.stack(
        [jnp.where(first_core, own, other), jnp.where(first_core, other, own)], 1
    ).reshape(2048, 768)
    wq_full = weights_all[:, :256]
    wkv_full = weights_all[:, 256:512]
    qa_all = spread(qa_own, "zl")
    kv_all = jnp.dot(enc_four, wkv_full, preferred_element_type=f32).astype(bf16)
    (parts,) = call(forward_kernel, [(4, 64, 896)], lengths, qa_all, kv_all)

    quarters = jnp.stack(
        [
            jnp.concatenate([dec_rows[:, at : at + 512], grad_rows[:, at : at + 512]], 1)
            for at in range(0, 2048, 512)
        ]
    )
    parts, quarters = together(parts, quarters)
    moved = lax.all_to_all(parts, "zl", 0, 0)
    x = lax.axis_index("x")
    rows_x = [lax.dynamic_index_in_dim(quarters, x, 0, keepdims=False)]
    for step in range(1, 4):
        part = lax.dynamic_index_in_dim(quarters, lax.rem(x + step, 4), 0, keepdims=False)
        rows_x.append(lax.ppermute(part, "x", [(i, (i + step) % 4) for i in range(4)]))
    moved, *rows_x = together(moved, *rows_x)
    heads, kv_part = call(backward_kernel, [(128, 256), (512, 256)], lengths, moved, qa_all, kv_all)

    keep, send = call(key_term_kernel, [(16, 64, 256)] * 2, core, kv_part, enc_four)
    kv_chip = join(keep, swap(send)).reshape(4, 256, 256)
    messages = jnp.concatenate([jnp.broadcast_to(heads[None], (4, 128, 256)), kv_chip], 1)
    moved_x = lax.all_to_all(messages, "x", 0, 0)
    sources = jnp.concatenate([core] + [lax.rem(x + 4 - step, 4).reshape(1) for step in range(4)])
    keep, send, kv_sum = call(
        head_term_kernel, [(256, 512), (256, 512), (256, 256)], sources, moved_x, *rows_x
    )
    sum_x = jnp.concatenate([join(keep, swap(send)), kv_sum], 1)
    sum_x, kv_part, heads = together(sum_x, kv_part, heads)

    sum_z = exchange(sum_x.reshape(4, 64, 768), "zh")
    dec_part = jnp.dot(heads[64:], wq_full.T, preferred_element_type=f32).astype(bf16)
    rest = [
        dec_part.reshape(64, 4, 512).transpose(1, 0, 2),
        kv_part.reshape(4, 2, 64, 256).transpose(0, 2, 1, 3).reshape(4, 64, 512),
    ]
    sum_z, *rest = together(sum_z, *rest)

    last = jnp.concatenate([jnp.broadcast_to(sum_z[None, :, 512:], (4, 64, 256)), *rest], 2)
    last = exchange(last, "y")
    mine = lax.all_gather(sum_z[:, :512], "zh", axis=0, tiled=True)
    copies = jnp.broadcast_to(mine[None], (4, 256, 512))
    copies, last = together(copies, last)
    mine = lax.all_to_all(copies, "x", 0, 0)
    kv_grad = jnp.concatenate([last[:, 768:1024], last[:, 1024:]], 0)
    enc_grad = jnp.dot(kv_grad, wkv_full.T, preferred_element_type=f32).astype(bf16)
    rows_zl = lax.all_gather(last[:, :768], "zl", axis=0)
    kv_weight_grad = jnp.sum(rows_zl[:, :, :256].astype(f32), 0)
    dec_zl = rows_zl[:, :, 256:].reshape(4, 64, 4, 128)
    dec_zl = lax.dynamic_index_in_dim(dec_zl, zl, 2, keepdims=False)
    dec_grad = jnp.sum(dec_zl.astype(f32), 0).astype(bf16)
    mine, rows_zl = together(mine, rows_zl)
    q_weight_grad, o_weight_grad = place(core, mine, swap(mine))
    return (dec_grad[None], enc_grad[None], q_weight_grad, kv_weight_grad, o_weight_grad)


def solution(mesh):
    fine = Mesh(mesh.devices.reshape(4, 4, 2, 4, 4), ("x", "zh", "co", "y", "zl"))
    pb = ("x", "zh", "co")
    row = ("y", "zl")
    placed = (
        P(pb, None, None),
        P(pb, row, None),
        P(pb, None),
        P(pb, row),
        P(pb, None),
        P(row, pb),
        P(pb, None, None),
    )
    return jax.shard_map(
        local,
        mesh=fine,
        in_specs=placed,
        out_specs=(
            P(pb, None, row),
            P(pb, row, None),
            P(None, row),
            P(pb, None),
            P(row, None),
        ),
        check_vma=False,
    )
```
